512 devices in a mesh: fsdp: 128 (over z, y, core), rep: 4 (over x).
Axes of the slice: x: 4, y: 8, z: 8, core: 2. Of those that a mesh axis runs over, the one named last changes fastest.
Arguments:
- gradients: float32 [192, 512, 512], P(None, 'fsdp', 'rep'), may hold values from -6 to 6
- moments: float32 [192, 512, 512], P(None, 'fsdp', 'rep')
- second_moments: float32 [192, 512, 512], P(None, 'fsdp', 'rep'), may hold values from 0.05 to 2
- factors: float32 [128, 4, 512, 512], P('fsdp', 'rep')
- owner_of: int32 [192], replicated, may hold values from 0 to 127, as said below
- slot_order: int32 [128, 2], replicated, may hold values from -1 to 191, as said below
Outputs:
- direction: float32 [192, 512, 512], P(None, 'fsdp', 'rep')
- new_moments: float32 [192, 512, 512], P(None, 'fsdp', 'rep')
- new_second_moments: float32 [192, 512, 512], P(None, 'fsdp', 'rep')
- new_factors: float32 [128, 4, 512, 512], P('fsdp', 'rep')
The draws below stay inside these ranges and needn't reach their ends.
Inputs may be any that keep to these rules, and one draw needn't show every extreme that they name: slot_order[o, k] is the block in slot k of owner o, or -1 if that slot is empty; every block stands in exactly one slot and every owner holds at least one block. owner_of[b] is the owner whose row of slot_order holds b.
All inputs are finite; a program needn't handle non-finite values.
Results may differ from the reference program's by a relative error of at most 0.0003.
Values sent between devices are 32-bit elements; how exact they have to be, the bound alone decides.
A program may use at most 64 MiB of HBM per device.

```python
import math
import jax
import jax.numpy as jnp
from jax import lax

BLOCK = 512
CAP = 2
NS_STEPS = 3
BLOCKS = 192
N_FSDP = 128


def assignment(key):
    owner_key, flip_key, block_key = jax.random.split(key, 3)
    extra = N_FSDP // 2
    owners = jax.random.permutation(owner_key, N_FSDP).astype(jnp.int32)
    flips = jax.random.randint(flip_key, (N_FSDP,), 0, 2).astype(jnp.int32)
    position = jnp.arange(N_FSDP, dtype=jnp.int32)
    first_slot = jnp.where(position < extra, 0, flips).astype(jnp.int32)
    place_owner = jnp.concatenate([owners, owners[:extra]])
    place_slot = jnp.concatenate([first_slot, jnp.ones((extra,), jnp.int32)])
    shuffled = jax.random.permutation(block_key, BLOCKS).astype(jnp.int32)
    table = jnp.full((N_FSDP, CAP), -1, jnp.int32).at[place_owner, place_slot].set(shuffled)
    owner_table = jnp.zeros((BLOCKS,), jnp.int32).at[shuffled].set(place_owner)
    return (owner_table, table)


def draw_owner_of(key, part):
    owner_table, table = assignment(key)
    return owner_table


def draw_slot_order(key, part):
    owner_table, table = assignment(key)
    return table


def draw_moments(key, part):
    key = jax.random.fold_in(key, 11)
    base_key, column_key = jax.random.split(key)
    shape = (BLOCKS, BLOCK, BLOCK)
    base = jax.random.normal(base_key, shape, jnp.float32)
    slope = 2.0
    rows = jnp.arange(BLOCK, dtype=jnp.float32) / BLOCK
    rising = 1.0 + slope * rows
    column = jnp.exp(jax.random.uniform(column_key, (BLOCKS, 1, BLOCK), jnp.float32, 0.0, math.log(4.0)))
    return 0.25 * base * rising[None, :, None] * column


def draw_factors(key, part):
    key = jax.random.fold_in(key, 17)
    diag_key, noise_key = jax.random.split(key)
    height, power = (2000.0, 0.6)
    spread = jax.random.uniform(diag_key, (N_FSDP, 2 * CAP, BLOCK), jnp.float32, 0.0, 1.0)
    diagonal = height * (BLOCK * spread + 1.0) ** (-power)
    floor_value = height * (BLOCK + 1.0) ** (-power)
    noise = jax.random.uniform(noise_key, (N_FSDP, 2 * CAP, BLOCK, BLOCK), jnp.float32, -1.0, 1.0)
    symmetric = (noise + jnp.swapaxes(noise, 2, 3)) * (0.25 * floor_value / BLOCK)
    identity = jnp.eye(BLOCK, dtype=jnp.float32)
    return symmetric * (1.0 - identity) + identity * diagonal[..., None]


def steps_of(own_key, dims, cuts, smallest, high):
    factor_of, own = 1.0, jax.random.fold_in(own_key, 6)
    for dim, shards_of in cuts:
        draws = jnp.exp(jax.random.uniform(jax.random.fold_in(own, dim), (shards_of,), jnp.float32, smallest / len(cuts), high / len(cuts)))
        factor_of = factor_of * jnp.repeat(draws, dims[dim] // shards_of).reshape([-1 if axis == dim else 1 for axis in range(len(dims))])
    return factor_of


def scatter_about(own_key, extent, scale, most, cuts=(), kind=jnp.bfloat16):
    factor_of = steps_of(own_key, extent, cuts, -0.22, 0.18) if cuts else 1.0
    array = jax.random.normal(own_key, extent, jnp.float32) * scale * factor_of
    return jnp.minimum(jnp.maximum(array, -most), most).astype(kind)


def setup_inputs(seed: int = 0) -> dict:
    key_list = jax.random.split(jax.random.key(seed), 7)
    return {
        "gradients": scatter_about(key_list[0], (BLOCKS, BLOCK, BLOCK), 1.0, 6.0, ((1, 128), (2, 4)), jnp.float32),
        "moments": draw_moments(jax.random.fold_in(key_list[6], 71), 0),
        "second_moments": jnp.clip(jnp.exp(math.log(2.0) - 3.6888794 * jax.random.uniform(key_list[2], (BLOCKS, BLOCK, BLOCK), jnp.float32) ** steps_of(key_list[2], (BLOCKS, BLOCK, BLOCK), ((1, 128), (2, 4)), -0.2, 0.2)), 0.05, 2.0),
        "factors": draw_factors(jax.random.fold_in(key_list[6], 71), 0),
        "owner_of": draw_owner_of(jax.random.fold_in(key_list[6], 71), 0),
        "slot_order": draw_slot_order(jax.random.fold_in(key_list[6], 71), 0),
    }


MOMENT_DECAY = 0.9
SECOND_DECAY = 0.95
FACTOR_DECAY = 0.95
DAMPING = 0.1
ADAM_EPSILON = 1e-08
NORM_EPSILON = 1e-06

def inverse_root(factor):
    highest = lax.Precision.HIGHEST
    identity = jnp.eye(factor.shape[0], dtype=jnp.float32)
    damped = factor + DAMPING * identity
    frobenius = jnp.sqrt(jnp.sum(damped * damped) + NORM_EPSILON)
    scaled = damped / frobenius
    root_est = identity
    for sweep in range(NS_STEPS):
        poly_term = (5.0 * identity - scaled) * 0.25
        if sweep == 0:
            root_est = poly_term * frobenius ** (-0.25)
        else:
            root_est = jnp.dot(root_est, poly_term, precision=highest, preferred_element_type=jnp.float32)
        if sweep + 1 < NS_STEPS:
            poly_square = jnp.dot(poly_term, poly_term, precision=highest, preferred_element_type=jnp.float32)
            poly_fourth = jnp.dot(poly_square, poly_square, precision=highest, preferred_element_type=jnp.float32)
            scaled = jnp.dot(poly_fourth, scaled, precision=highest, preferred_element_type=jnp.float32)
    return root_est

def reference(gradients, moments, second_moments, factors, owner_of, slot_order):
    highest = lax.Precision.HIGHEST
    new_moment = MOMENT_DECAY * moments + (1.0 - MOMENT_DECAY) * gradients
    new_second = SECOND_DECAY * second_moments + (1.0 - SECOND_DECAY) * gradients * gradients
    adam_step = new_moment / (jnp.sqrt(new_second) + ADAM_EPSILON)
    adam_sq = lax.optimization_barrier(jnp.sum(adam_step * adam_step, axis=(1, 2)))
    capacity = slot_order.shape[1]
    block_ids = jnp.arange(BLOCKS, dtype=jnp.int32)
    matches = slot_order[owner_of] == block_ids[:, None]
    slot_of = lax.optimization_barrier(jnp.sum(jnp.where(matches, jnp.arange(capacity, dtype=jnp.int32)[None, :], 0), axis=1)).astype(jnp.int32)
    left_old = factors[owner_of, 2 * slot_of]
    right_old = factors[owner_of, 2 * slot_of + 1]

    def one_block(block_items):
        grad_block, left_prev, right_prev, adam_total = block_items
        left_gram = jnp.dot(grad_block, grad_block.T, precision=highest, preferred_element_type=jnp.float32)
        right_gram = jnp.dot(grad_block.T, grad_block, precision=highest, preferred_element_type=jnp.float32)
        left_new = FACTOR_DECAY * left_prev + (1.0 - FACTOR_DECAY) * left_gram
        right_new = FACTOR_DECAY * right_prev + (1.0 - FACTOR_DECAY) * right_gram
        left_root = inverse_root(left_new)
        right_root = inverse_root(right_new)
        right_applied = jnp.dot(grad_block, right_root, precision=highest, preferred_element_type=jnp.float32)
        shampoo = jnp.dot(left_root, right_applied, precision=highest, preferred_element_type=jnp.float32)
        shampoo_total = jnp.sum(shampoo * shampoo)
        grafted = shampoo * (jnp.sqrt(adam_total) / jnp.sqrt(shampoo_total + NORM_EPSILON))
        return (left_new, right_new, grafted)
    left_new, right_new, direction = lax.map(one_block, (gradients, left_old, right_old, adam_sq))
    new_factors = FACTOR_DECAY * factors
    new_factors = new_factors.at[owner_of, 2 * slot_of].set(left_new)
    new_factors = new_factors.at[owner_of, 2 * slot_of + 1].set(right_new)
    return (direction, new_moment, new_second, new_factors)
```

```python
import jax
import jax.numpy as jnp
from jax import lax
from jax.experimental import pallas as pl
from jax.experimental.pallas import tpu as pltpu
from jax.sharding import PartitionSpec as P

MOMENT_DECAY = 0.9
SECOND_DECAY = 0.95
FACTOR_DECAY = 0.95
DAMPING = 0.1
ADAM_EPSILON = 1e-08
NORM_EPSILON = 1e-06

BLOCK = 512
OWNERS = 128
BLOCKS = 192
MESH = pl.DeviceIdType.MESH
f32 = jnp.float32
bf16 = jnp.bfloat16


def split(x):
    hi = x.astype(bf16)
    return hi, (x - hi.astype(f32)).astype(bf16)


def mm(a, b, dims=((1,), (0,))):
    (ah, al), (bh, bl) = a, b

    def dot(x, y):
        return lax.dot_general(x, y, (dims, ((), ())), preferred_element_type=f32)

    return dot(ah, bh) + (dot(ah, bl) + dot(al, bh))


def damp(factor, eye):
    damped = factor + DAMPING * eye
    frobenius = jnp.sqrt(jnp.sum(damped * damped, keepdims=True) + NORM_EPSILON)
    return damped * (1.0 / frobenius), frobenius


def root_steps(factor, eye):
    m, c = damp(factor, eye)
    ms = split(m)
    n = mm(ms, ms)
    q = split(1.5625 * eye - 0.625 * m + 0.0625 * n)
    yield
    q = split(mm(q, q))
    yield
    m1 = mm(q, ms)
    m1s = split(m1)
    yield
    n1 = mm(m1s, m1s)
    p = split(1.5625 * eye - 0.625 * m1 + 0.0625 * n1)
    w = split(1.25 * m1 - 0.25 * n1)
    yield
    p = split(mm(p, p))
    yield
    y = mm(p, w)
    u = split(1.5625 * eye - 0.3125 * m1 - 0.25 * y)
    t0 = split((1.25 * eye - 0.25 * m) * lax.rsqrt(jnp.sqrt(c)))
    yield
    yield split(mm(t0, u))


def run(gen):
    last = None
    for last in gen:
        pass
    return last


def remote(src, dst, send, recv, device):
    return pltpu.make_async_remote_copy(
        src_ref=src, dst_ref=dst, send_sem=send, recv_sem=recv, device_id=device, device_id_type=MESH
    )


def wrap(v, n):
    return jnp.where(v >= n, v - n, v)


def kernel(
    slot_ref, owner_ref, g_ref, m_ref, v_ref, f_ref,
    dir_ref, nm_ref, nv_ref, nf_ref,
    pay, gq, other, fresh, xq, xs, ret, eye_ref, g_full, sums, part, ga, gz, gx,
    stage, send1, recv1, fsend, frecv, usend, urecv, spsend, sprecv, send2, recv2,
    asend, arecv,
):
    me = lax.axis_index("fsdp")
    rep = lax.axis_index("rep")
    z = me // 16
    yc = me - z * 16
    site = lax.rem(rep, 2) == 0
    slot = rep // 2

    barrier = pltpu.get_barrier_semaphore()

    def signal(sem, d, r):
        pl.semaphore_signal(sem, inc=1, device_id=(d, r), device_id_type=MESH)

    for t in range(4):
        for s in range(0 if t else 1, 16):
            signal(barrier, z * 16 + wrap(yc + s, 16), wrap(rep + t, 4))
    for s in range(1, 8):
        signal(barrier, wrap(z + s, 8) * 16 + yc, rep)

    def pick(o, carry):
        for k in range(2):
            b = slot_ref[2 * o + k]
            chunk = g_ref[jnp.maximum(b, 0)]
            pay[k, o] = jnp.where(b >= 0, chunk, 0.0)
        return carry

    lax.fori_loop(0, OWNERS, pick, 0, unroll=8)

    pl.semaphore_wait(barrier, 70)
    for s in range(1, 8):
        signal(stage, wrap(z + s, 8) * 16 + yc, rep)
    pl.semaphore_wait(stage, 7)

    def send(s, carry):
        d = lax.rem(me + s * 37, OWNERS)
        for k in range(2):
            remote(pay.at[k, d], gq.at[rep, me // 2, lax.rem(me, 2)], send1, recv1.at[rep], (d, 2 * k)).start()
        return carry

    lax.fori_loop(1, OWNERS, send, 0, unroll=4)
    for k in range(2):
        own_chunk = gq.at[rep, me // 2, lax.rem(me, 2)]

        @pl.when(rep != 2 * k)
        def _():
            remote(pay.at[k, me], own_chunk, send1, recv1.at[rep], (me, 2 * k)).start()

        @pl.when(rep == 2 * k)
        def _():
            pltpu.make_async_copy(pay.at[k, me], own_chunk, recv1.at[rep]).start()

    @pl.when(jnp.logical_not(site))
    def _():
        remote(f_ref, other, fsend, frecv, (me, rep - 1)).start()

    grad = g_ref[...]
    new_m = MOMENT_DECAY * m_ref[...] + (1.0 - MOMENT_DECAY) * grad
    new_v = SECOND_DECAY * v_ref[...] + (1.0 - SECOND_DECAY) * grad * grad
    nm_ref[...] = new_m
    nv_ref[...] = new_v
    adam = new_m / (jnp.sqrt(new_v) + ADAM_EPSILON)
    rows = jnp.sum(adam * adam, axis=1)
    part[...] = jnp.zeros_like(part)
    part[0:BLOCKS, :] = rows
    total = lax.dot_general(
        jnp.ones((8, 128), f32), part[...], (((1,), (1,)), ((), ())),
        precision=lax.Precision.HIGHEST, preferred_element_type=f32,
    )[0:1]

    def share(buf, step, here, n, device):
        buf[here] = sums_of[0]
        for s in range(1, n):
            remote(buf.at[here], buf.at[here], asend.at[step], arecv.at[step], device(s)).start()
        some = buf.at[pl.ds(0, n - 1)]
        pltpu.make_async_copy(some, some, asend.at[step]).wait()
        pltpu.make_async_copy(some, some, arecv.at[step]).wait()
        out = buf[0]
        for s in range(1, n):
            out = out + buf[s]
        sums_of[0] = out

    sums_of = [total]
    share(ga, 0, yc, 16, lambda s: (z * 16 + wrap(yc + s, 16), rep))
    share(gz, 1, z, 8, lambda s: (wrap(z + s, 8) * 16 + yc, rep))
    share(gx, 2, rep, 4, lambda s: (me, wrap(rep + s, 4)))
    sums[...] = sums_of[0]

    pltpu.make_async_copy(pay.at[:, pl.ds(0, 127)], pay.at[:, pl.ds(0, 127)], send1).wait()
    for k in range(2):
        @pl.when(rep != 2 * k)
        def _():
            pltpu.make_async_copy(pay.at[k, 0], pay.at[k, 0], send1).wait()

    @pl.when(site)
    def _():
        row = lax.broadcasted_iota(jnp.int32, (BLOCK, BLOCK), 0)
        col = lax.broadcasted_iota(jnp.int32, (BLOCK, BLOCK), 1)
        eye_ref[...] = jnp.where(row == col, 1.0, 0.0)
        for q in range(4):
            pltpu.make_async_copy(gq.at[q], gq.at[q], recv1.at[q]).wait()
        for q in range(4):
            both = jnp.concatenate([gq[q, :, 0], gq[q, :, 1]], axis=1)
            g_full[:, q * 128 : (q + 1) * 128] = both.reshape(BLOCK, 128)
        gs = split(g_full[...])
        left_gram = mm(gs, gs, ((1,), (1,)))
        left = FACTOR_DECAY * f_ref[...] + (1.0 - FACTOR_DECAY) * left_gram
        nf_ref[...] = left
        left_root = run(root_steps(left, eye_ref[...]))
        applied = split(mm(left_root, gs))
        right_gram = mm(gs, gs, ((0,), (0,)))
        remote(f_ref, other, fsend, frecv, (me, rep + 1)).wait_recv()
        right = FACTOR_DECAY * other[...] + (1.0 - FACTOR_DECAY) * right_gram
        fresh[...] = right
        remote(fresh, nf_ref, usend, urecv, (me, rep + 1)).start()
        right_root = run(root_steps(right, eye_ref[...]))
        shampoo = mm(applied, right_root)
        b = slot_ref[2 * me + slot]
        lane = lax.broadcasted_iota(jnp.int32, sums.shape, 1)
        adam_total = jnp.sum(jnp.where(lane == b, sums[...], 0.0), keepdims=True)
        shampoo_total = jnp.sum(shampoo * shampoo, keepdims=True)
        scale = jnp.sqrt(adam_total) / jnp.sqrt(shampoo_total + NORM_EPSILON)
        for q in range(4):
            part_q = (shampoo[:, q * 128 : (q + 1) * 128] * scale).reshape(64, 8, 128)
            xq[q, :, 0] = part_q[:, 0:4]
            xq[q, :, 1] = part_q[:, 4:8]
        for c in range(4):
            @pl.when(rep != c)
            def _():
                remote(xq.at[c], xs.at[slot], spsend, sprecv.at[slot], (me, c)).start()

            @pl.when(rep == c)
            def _():
                pltpu.make_async_copy(xq.at[c], xs.at[slot], sprecv.at[slot]).start()

    for k in range(2):
        pltpu.make_async_copy(xs.at[k], xs.at[k], sprecv.at[k]).wait()

    def give(s, carry):
        d = lax.rem(me + s * 37, OWNERS)
        remote(xs.at[:, d // 2, lax.rem(d, 2)], ret.at[:, me], send2, recv2, (d, rep)).start()
        return carry

    lax.fori_loop(1, OWNERS, give, 0, unroll=4)
    pltpu.make_async_copy(xs.at[:, me // 2, lax.rem(me, 2)], ret.at[:, me], recv2).start()
    pltpu.make_async_copy(pay.at[:, pl.ds(0, 127)], pay.at[:, pl.ds(0, 127)], send2).wait()
    pltpu.make_async_copy(ret, ret, recv2).wait()

    def place(b, carry):
        o = owner_ref[b]
        k = jnp.where(slot_ref[2 * o] == b, 0, 1)
        dir_ref[b] = ret[k, o]
        return carry

    lax.fori_loop(0, BLOCKS, place, 0, unroll=8)

    @pl.when(site)
    def _():
        remote(fresh, nf_ref, usend, urecv, (me, rep + 1)).wait_send()
        pltpu.make_async_copy(xq.at[pl.ds(0, 3)], xq.at[pl.ds(0, 3)], spsend).wait()

    @pl.when(jnp.logical_not(site))
    def _():
        remote(f_ref, other, fsend, frecv, (me, rep - 1)).wait_send()
        remote(fresh, nf_ref, usend, urecv, (me, rep - 1)).wait_recv()


def shards(gradients, moments, second_moments, factors, owner_of, slot_order):
    vmem = pl.BlockSpec(memory_space=pltpu.VMEM)
    smem = pl.BlockSpec(memory_space=pltpu.SMEM)
    part = jax.ShapeDtypeStruct(gradients.shape, f32)
    chunks = lambda n: pltpu.VMEM((n, OWNERS, 4, 128), f32)
    halves = lambda n: pltpu.VMEM((n, 64, 2, 4, 128), f32)
    square = pltpu.VMEM((BLOCK, BLOCK), f32)
    dma = pltpu.SemaphoreType.DMA
    direction, new_m, new_v, new_f = pl.pallas_call(
        kernel,
        out_shape=(part, part, part, jax.ShapeDtypeStruct((BLOCK, BLOCK), f32)),
        in_specs=[smem, smem, vmem, vmem, vmem, vmem],
        out_specs=(vmem, vmem, vmem, vmem),
        scratch_shapes=[
            chunks(2), halves(4), square, square, halves(4), halves(2), chunks(2), square, square,
            pltpu.VMEM((1, 256), f32), pltpu.VMEM((256, 128), f32),
            pltpu.VMEM((16, 1, 256), f32), pltpu.VMEM((8, 1, 256), f32), pltpu.VMEM((4, 1, 256), f32),
            pltpu.SemaphoreType.REGULAR, dma, dma((4,)), dma, dma, dma, dma, dma, dma((2,)), dma, dma,
            dma((3,)), dma((3,)),
        ],
        compiler_params=pltpu.CompilerParams(
            collective_id=0, has_side_effects=True, vmem_limit_bytes=56 << 20
        ),
    )(slot_order.reshape(-1), owner_of, gradients, moments, second_moments, factors.reshape(BLOCK, BLOCK))
    return direction, new_m, new_v, new_f[None, None]


def solution(mesh):
    split_blocks = P(None, "fsdp", "rep")
    return jax.shard_map(
        shards,
        mesh=mesh,
        in_specs=(split_blocks, split_blocks, split_blocks, P("fsdp", "rep", None, None), P(), P()),
        out_specs=(split_blocks, split_blocks, split_blocks, P("fsdp", "rep", None, None)),
        check_vma=False,
    )
```

```python
import functools

import jax
import jax.numpy as jnp
from jax import lax
from jax.experimental import pallas as pl
from jax.experimental.pallas import tpu as pltpu
from jax.sharding import PartitionSpec as P

MOMENT_DECAY = 0.9
SECOND_DECAY = 0.95
FACTOR_DECAY = 0.95
DAMPING = 0.1
ADAM_EPSILON = 1e-08
NORM_EPSILON = 1e-06

BLOCK = 512
OWNERS = 128
BLOCKS = 192
MESH = pl.DeviceIdType.MESH
DIRECT = (0, 4)
PHASES = ((1, 2, 3), (5, 6, 7))
RELAYED = 16 * sum(len(p) for p in PHASES)
f32 = jnp.float32
bf16 = jnp.bfloat16


def split(x):
    hi = x.astype(bf16)
    return hi, (x - hi.astype(f32)).astype(bf16)


def mm(a, b, dims=((1,), (0,))):
    (ah, al), (bh, bl) = a, b

    def dot(x, y):
        return lax.dot_general(x, y, (dims, ((), ())), preferred_element_type=f32)

    return dot(ah, bh) + (dot(ah, bl) + dot(al, bh))


def damp(factor, eye):
    damped = factor + DAMPING * eye
    frobenius = jnp.sqrt(jnp.sum(damped * damped, keepdims=True) + NORM_EPSILON)
    return damped * (1.0 / frobenius), frobenius


def root_steps(factor, eye):
    m, c = damp(factor, eye)
    ms = split(m)
    n = mm(ms, ms)
    q = split(1.5625 * eye - 0.625 * m + 0.0625 * n)
    yield
    q = split(mm(q, q))
    yield
    m1 = mm(q, ms)
    m1s = split(m1)
    yield
    n1 = mm(m1s, m1s)
    p = split(1.5625 * eye - 0.625 * m1 + 0.0625 * n1)
    w = split(1.25 * m1 - 0.25 * n1)
    yield
    p = split(mm(p, p))
    yield
    y = mm(p, w)
    u = split(1.5625 * eye - 0.3125 * m1 - 0.25 * y)
    t0 = split((1.25 * eye - 0.25 * m) * lax.rsqrt(jnp.sqrt(c)))
    yield
    yield split(mm(t0, u))


def run(gen):
    last = None
    for last in gen:
        pass
    return last


def remote(src, dst, send, recv, device):
    return pltpu.make_async_remote_copy(
        src_ref=src, dst_ref=dst, send_sem=send, recv_sem=recv, device_id=device, device_id_type=MESH
    )


def wrap(v, n):
    return jnp.where(v >= n, v - n, v)


def kernel(
    slot_ref, owner_ref, g_ref, m_ref, v_ref, f_ref,
    dir_ref, nm_ref, nv_ref, nf_ref,
    pay, gq, other, gram, xq, xs, ret, eye_ref, g_full, sums, part, ga, gz, gx,
    inside, stage2, stage3, stage4, go2, go3,
    send1, recv1, fsend, frecv, usend, urecv, spsend, sprecv, send2, recv2, asend, arecv,
):
    me = lax.axis_index("fsdp")
    rep = lax.axis_index("rep")
    z = me // 16
    yc = me - z * 16
    site = lax.rem(rep, 2) == 0
    odd = jnp.logical_not(site)
    slot = rep // 2
    twin = wrap(rep + 2, 4)

    barrier = pltpu.get_barrier_semaphore()

    def signal(sem, d, r):
        pl.semaphore_signal(sem, inc=1, device_id=(d, r), device_id_type=MESH)

    @pl.when(site)
    def _():
        signal(barrier, me, rep + 1)
        for t in range(2):
            for s in range(0 if t else 1, 16):
                signal(barrier, z * 16 + wrap(yc + s, 16), wrap(rep + 2 * t, 4))
            for s in range(1, 8):
                signal(barrier, wrap(z + s, 8) * 16 + yc, wrap(rep + 2 * t, 4))

    @pl.when(odd)
    def _():
        pl.semaphore_wait(barrier, 1)
        remote(f_ref, other, fsend, frecv, (me, rep - 1)).start()
        signal(inside, me, rep - 1)

    def pick(o, carry):
        for k in range(2):
            b = slot_ref[k, o]
            chunk = g_ref[jnp.maximum(b, 0)]
            pay[k, o] = jnp.where(b >= 0, chunk, 0.0)
        return carry

    lax.fori_loop(0, OWNERS, pick, 0, unroll=8)

    @pl.when(site)
    def _():
        pl.semaphore_wait(barrier, 45)
        pl.semaphore_wait(inside, 1)
        for s in range(1, 16):
            signal(stage2, z * 16 + wrap(yc + s, 16), rep)
        pl.semaphore_wait(stage2, 15)
        signal(go2, me, rep + 1)

    @pl.when(odd)
    def _():
        pl.semaphore_wait(go2, 1)

    def send(s, carry):
        d = lax.rem(me + s * 37, OWNERS)
        for k in range(2):
            remote(pay.at[k, d], gq.at[rep, me // 2, lax.rem(me, 2)], send1, recv1.at[rep], (d, 2 * k)).start()
        return carry

    lax.fori_loop(1, OWNERS, send, 0, unroll=4)
    for k in range(2):
        own_chunk = gq.at[rep, me // 2, lax.rem(me, 2)]

        @pl.when(rep != 2 * k)
        def _():
            remote(pay.at[k, me], own_chunk, send1, recv1.at[rep], (me, 2 * k)).start()

        @pl.when(rep == 2 * k)
        def _():
            pltpu.make_async_copy(pay.at[k, me], own_chunk, recv1.at[rep]).start()

    @pl.when(site)
    def _():
        for s in range(1, 8):
            signal(stage3, wrap(z + s, 8) * 16 + yc, rep)
        pl.semaphore_wait(stage3, 7)
        signal(stage4, me, twin)
        pl.semaphore_wait(stage4, 1)
        signal(go3, me, rep + 1)

    @pl.when(odd)
    def _():
        pl.semaphore_wait(go3, 1)

    grad = g_ref[...]
    new_m = MOMENT_DECAY * m_ref[...] + (1.0 - MOMENT_DECAY) * grad
    new_v = SECOND_DECAY * v_ref[...] + (1.0 - SECOND_DECAY) * grad * grad
    nm_ref[...] = new_m
    nv_ref[...] = new_v
    adam = new_m / (jnp.sqrt(new_v) + ADAM_EPSILON)
    rows = jnp.sum(adam * adam, axis=1)
    part[...] = jnp.zeros_like(part)
    part[0:BLOCKS, :] = rows
    total = lax.dot_general(
        jnp.ones((8, 128), f32), part[...], (((1,), (1,)), ((), ())),
        precision=lax.Precision.HIGHEST, preferred_element_type=f32,
    )[0:1]

    def z_peer(s):
        return wrap(z + s, 8) * 16 + yc

    def y_peer(s):
        return z * 16 + wrap(yc + s, 16)

    def share(buf, step, here, n, value, peer):
        buf[here] = value
        for s in range(1, n):
            remote(buf.at[here], buf.at[here], asend.at[step], arecv.at[step], (peer(s), rep)).start()

    def shared(buf, step, n):
        some = buf.at[pl.ds(0, n - 1)]
        pltpu.make_async_copy(some, some, asend.at[step]).wait()
        pltpu.make_async_copy(some, some, arecv.at[step]).wait()
        return functools.reduce(lambda x, y: x + y, [buf[s] for s in range(n)])

    share(ga, 0, yc, 16, total, y_peer)

    def share_z():
        share(gz, 1, z, 8, shared(ga, 0, 16), z_peer)

    def share_x():
        gx[rep] = shared(gz, 1, 8)

        @pl.when(odd)
        def _():
            for k in range(2):
                remote(gx.at[rep], gx.at[rep], asend.at[2], arecv.at[2], (me, 2 * k)).start()

        @pl.when(site)
        def _():
            remote(gx.at[rep], gx.at[rep], asend.at[3], arecv.at[2], (me, twin)).start()

    @pl.when(odd)
    def _():
        share_z()
        share_x()

    def units(n, sem):
        while n > 0:
            some = xq.at[0, pl.ds(0, min(n, 64))]
            pltpu.make_async_copy(some, some, sem).wait()
            n -= 64

    def group(dz):
        return pl.ds(wrap(z + dz, 8) * 8, 8)

    def each(dzs, act):
        for dz in dzs:
            base = wrap(z + dz, 8) * 16
            if dz == 0:
                act(me, True)

            def body(j, carry):
                act(base + wrap(yc + j, 16), False)
                return carry

            lax.fori_loop(1 if dz == 0 else 0, 16, body, 0, unroll=4 if dz else 3)

    @pl.when(site)
    def _():
        row = lax.broadcasted_iota(jnp.int32, (BLOCK, BLOCK), 0)
        col = lax.broadcasted_iota(jnp.int32, (BLOCK, BLOCK), 1)
        eye_ref[...] = jnp.where(row == col, 1.0, 0.0)
        for q in range(4):
            pltpu.make_async_copy(gq.at[q], gq.at[q], recv1.at[q]).wait()
        for q in range(4):
            both = jnp.concatenate([gq[q, :, 0], gq[q, :, 1]], axis=1)
            g_full[:, q * 128 : (q + 1) * 128] = both.reshape(BLOCK, 128)
        gs = split(g_full[...])
        gram[...] = mm(gs, gs, ((0,), (0,)))
        for i in range(4):
            panel = gram.at[pl.ds(128 * i, 128), pl.ds(128 * i, BLOCK - 128 * i)]
            there = other.at[pl.ds(128 * i, 128), pl.ds(128 * i, BLOCK - 128 * i)]
            remote(panel, there, usend.at[i], urecv.at[i], (me, rep + 1)).start()
        left_gram = mm(gs, gs, ((1,), (1,)))
        left = FACTOR_DECAY * f_ref[...] + (1.0 - FACTOR_DECAY) * left_gram
        nf_ref[...] = left
        share_z()
        left_root = run(root_steps(left, eye_ref[...]))
        applied = split(mm(left_root, gs))
        share_x()
        remote(f_ref, other, fsend, frecv, (me, rep + 1)).wait_recv()
        right = FACTOR_DECAY * other[...] + (1.0 - FACTOR_DECAY) * gram[...]
        right_root = run(root_steps(right, eye_ref[...]))
        shampoo = mm(applied, right_root)
        remote(gx.at[rep], gx.at[rep], asend.at[3], arecv.at[2], (me, twin)).wait_send()
        pltpu.make_async_copy(gx.at[pl.ds(0, 3)], gx.at[pl.ds(0, 3)], arecv.at[2]).wait()
        sums[...] = gx[0] + gx[1] + gx[2] + gx[3]
        b = slot_ref[slot, me]
        lane = lax.broadcasted_iota(jnp.int32, sums.shape, 1)
        adam_total = jnp.sum(jnp.where(lane == b, sums[...], 0.0), keepdims=True)
        shampoo_total = jnp.sum(shampoo * shampoo, keepdims=True)
        scale = jnp.sqrt(adam_total) / jnp.sqrt(shampoo_total + NORM_EPSILON)
        for q in range(4):
            part_q = (shampoo[:, q * 128 : (q + 1) * 128] * scale).reshape(64, 8, 128)
            xq[q, :, 0] = part_q[:, 0:4]
            xq[q, :, 1] = part_q[:, 4:8]
        for phase, dzs in enumerate(PHASES):
            for dz in dzs:
                for c in (1, 3):
                    remote(xq.at[c, group(dz)], xs.at[slot, group(dz)], spsend, sprecv.at[slot, phase], (me, c)).start()

        def own(d, same):
            chunk = xq.at[rep, d // 2, lax.rem(d, 2)]
            if same:
                pltpu.make_async_copy(chunk, ret.at[slot, me], recv2).start()
            else:
                remote(chunk, ret.at[slot, me], send2, recv2, (d, rep)).start()

        def across(d, same):
            remote(xq.at[twin, d // 2, lax.rem(d, 2)], ret.at[slot, me], send2, recv2, (d, twin)).start()

        def aside(d, same):
            for c in (1, 3):
                remote(xq.at[c, d // 2, lax.rem(d, 2)], ret.at[slot, me], send2, recv2, (d, c)).start()

        each(range(8), own)
        each(range(8), across)
        each(DIRECT, aside)
        units(RELAYED, spsend)
        units(127 + 16 * len(DIRECT), send2)
        one = pay.at[0, 0]
        pltpu.make_async_copy(one, one, send2).wait()

    @pl.when(odd)
    def _():
        for i in range(4):
            there = other.at[pl.ds(128 * i, 128), pl.ds(128 * i, BLOCK - 128 * i)]
            remote(there, there, usend.at[i], urecv.at[i], (me, rep - 1)).wait_recv()
        for i in range(4):
            for j in range(4):
                a, b = slice(128 * i, 128 * i + 128), slice(128 * j, 128 * j + 128)
                square = other[a, b] if i <= j else other[b, a].T
                nf_ref[a, b] = FACTOR_DECAY * f_ref[a, b] + (1.0 - FACTOR_DECAY) * square

        def give(d, same):
            chunk = xs.at[:, d // 2, lax.rem(d, 2)]
            if same:
                pltpu.make_async_copy(chunk, ret.at[:, me], recv2).start()
            else:
                remote(chunk, ret.at[:, me], send2, recv2, (d, rep)).start()

        for phase, dzs in enumerate(PHASES):
            some = xs.at[0, pl.ds(0, 8 * len(dzs))]
            for k in range(2):
                pltpu.make_async_copy(some, some, sprecv.at[k, phase]).wait()
            each(dzs, give)
        units(RELAYED, send2)
        pair = gx.at[pl.ds(0, 2)]
        pltpu.make_async_copy(pair, pair, asend.at[2]).wait()
        remote(f_ref, other, fsend, frecv, (me, rep - 1)).wait_send()

    pltpu.make_async_copy(pay.at[:, pl.ds(0, 127)], pay.at[:, pl.ds(0, 127)], send1).wait()
    for k in range(2):
        @pl.when(rep != 2 * k)
        def _():
            pltpu.make_async_copy(pay.at[k, 0], pay.at[k, 0], send1).wait()

    pltpu.make_async_copy(ret, ret, recv2).wait()

    def place(b, carry):
        o = owner_ref[b]
        k = jnp.where(slot_ref[0, o] == b, 0, 1)
        dir_ref[b] = ret[k, o]
        return carry

    lax.fori_loop(0, BLOCKS, place, 0, unroll=8)

    @pl.when(site)
    def _():
        for i in range(4):
            panel = gram.at[pl.ds(128 * i, 128), pl.ds(128 * i, BLOCK - 128 * i)]
            remote(panel, panel, usend.at[i], urecv.at[i], (me, rep + 1)).wait_send()


def shards(gradients, moments, second_moments, factors, owner_of, slot_order):
    vmem = pl.BlockSpec(memory_space=pltpu.VMEM)
    smem = pl.BlockSpec(memory_space=pltpu.SMEM)
    part = jax.ShapeDtypeStruct(gradients.shape, f32)
    chunks = lambda n: pltpu.VMEM((n, OWNERS, 4, 128), f32)
    halves = lambda n: pltpu.VMEM((n, 64, 2, 4, 128), f32)
    square = pltpu.VMEM((BLOCK, BLOCK), f32)
    dma = pltpu.SemaphoreType.DMA
    regular = pltpu.SemaphoreType.REGULAR
    direction, new_m, new_v, new_f = pl.pallas_call(
        kernel,
        out_shape=(part, part, part, jax.ShapeDtypeStruct((BLOCK, BLOCK), f32)),
        in_specs=[smem, smem, vmem, vmem, vmem, vmem],
        out_specs=(vmem, vmem, vmem, vmem),
        scratch_shapes=[
            chunks(2), halves(4), square, square, halves(4), halves(2), chunks(2), square, square,
            pltpu.VMEM((1, 256), f32), pltpu.VMEM((256, 128), f32),
            pltpu.VMEM((16, 1, 256), f32), pltpu.VMEM((8, 1, 256), f32), pltpu.VMEM((4, 1, 256), f32),
            regular, regular, regular, regular, regular, regular,
            dma, dma((4,)), dma, dma, dma((4,)), dma((4,)), dma, dma((2, 2)), dma, dma, dma((4,)), dma((3,)),
        ],
        compiler_params=pltpu.CompilerParams(
            collective_id=0, has_side_effects=True, vmem_limit_bytes=56 << 20
        ),
    )(slot_order.T, owner_of, gradients, moments, second_moments, factors.reshape(BLOCK, BLOCK))
    return direction, new_m, new_v, new_f[None, None]


def solution(mesh):
    split_blocks = P(None, "fsdp", "rep")
    return jax.shard_map(
        shards,
        mesh=mesh,
        in_specs=(split_blocks, split_blocks, split_blocks, P("fsdp", "rep", None, None), P(), P()),
        out_specs=(split_blocks, split_blocks, split_blocks, P("fsdp", "rep", None, None)),
        check_vma=False,
    )
```

```python
import functools

import jax
import jax.numpy as jnp
from jax import lax
from jax.experimental import pallas as pl
from jax.experimental.pallas import tpu as pltpu
from jax.sharding import PartitionSpec as P

MOMENT_DECAY = 0.9
SECOND_DECAY = 0.95
FACTOR_DECAY = 0.95
DAMPING = 0.1
ADAM_EPSILON = 1e-08
NORM_EPSILON = 1e-06

BLOCK = 512
OWNERS = 128
BLOCKS = 192
MESH = pl.DeviceIdType.MESH
DIRECT = (0, 4)
PHASES = ((1, 2, 3), (5, 6, 7))
RELAYED = 16 * sum(len(p) for p in PHASES)
f32 = jnp.float32
bf16 = jnp.bfloat16


def split(x):
    hi = x.astype(bf16)
    return hi, (x - hi.astype(f32)).astype(bf16)


def mm(a, b, dims=((1,), (0,))):
    (ah, al), (bh, bl) = a, b

    def dot(x, y):
        return lax.dot_general(x, y, (dims, ((), ())), preferred_element_type=f32)

    return dot(ah, bh) + (dot(ah, bl) + dot(al, bh))


def damp(factor, eye):
    damped = factor + DAMPING * eye
    frobenius = jnp.sqrt(jnp.sum(damped * damped, keepdims=True) + NORM_EPSILON)
    return damped * (1.0 / frobenius), frobenius


def root_steps(factor, eye):
    m, c = damp(factor, eye)
    ms = split(m)
    n = mm(ms, ms)
    q = split(1.5625 * eye - 0.625 * m + 0.0625 * n)
    yield
    q = split(mm(q, q))
    yield
    m1 = mm(q, ms)
    m1s = split(m1)
    yield
    n1 = mm(m1s, m1s)
    p = split(1.5625 * eye - 0.625 * m1 + 0.0625 * n1)
    w = split(1.25 * m1 - 0.25 * n1)
    yield
    p = split(mm(p, p))
    yield
    y = mm(p, w)
    u = split(1.5625 * eye - 0.3125 * m1 - 0.25 * y)
    t0 = split((1.25 * eye - 0.25 * m) * lax.rsqrt(jnp.sqrt(c)))
    yield
    yield split(mm(t0, u))


def run(gen):
    last = None
    for last in gen:
        pass
    return last


def remote(src, dst, send, recv, device):
    return pltpu.make_async_remote_copy(
        src_ref=src, dst_ref=dst, send_sem=send, recv_sem=recv, device_id=device, device_id_type=MESH
    )


def wrap(v, n):
    return jnp.where(v >= n, v - n, v)


def kernel(
    slot_ref, owner_ref, g_hbm, m_hbm, v_hbm, f_hbm,
    dir_hbm, nm_hbm, nv_hbm, nf_hbm,
    g_ref, m_ref, v_ref, f_ref, dir_ref, nm_ref, nv_ref, nf_ref, where_ref,
    pay, gq, other, gram, xq, xs, ret, eye_ref, g_full, sums, part, ga, gz, gx,
    inside, stage2, stage3, stage4, go2, go3,
    send1, recv1, fsend, frecv, usend, urecv, spsend, sprecv, send2, recv2, asend, arecv, loads, stores,
):
    me = lax.axis_index("fsdp")
    rep = lax.axis_index("rep")
    z = me // 16
    yc = me - z * 16
    site = lax.rem(rep, 2) == 0
    odd = jnp.logical_not(site)
    slot = rep // 2
    twin = wrap(rep + 2, 4)

    barrier = pltpu.get_barrier_semaphore()

    def signal(sem, d, r):
        pl.semaphore_signal(sem, inc=1, device_id=(d, r), device_id_type=MESH)

    @pl.when(site)
    def _():
        signal(barrier, me, rep + 1)
        for t in range(2):
            for s in range(0 if t else 1, 16):
                signal(barrier, z * 16 + wrap(yc + s, 16), wrap(rep + 2 * t, 4))
            for s in range(1, 8):
                signal(barrier, wrap(z + s, 8) * 16 + yc, wrap(rep + 2 * t, 4))

    arrays = ((g_hbm, g_ref), (m_hbm, m_ref), (v_hbm, v_ref), (f_hbm, f_ref))
    load = [pltpu.make_async_copy(a, b, loads.at[i]) for i, (a, b) in enumerate(arrays)]
    arrays = ((dir_ref, dir_hbm), (nm_ref, nm_hbm), (nv_ref, nv_hbm), (nf_ref, nf_hbm))
    store = [pltpu.make_async_copy(a, b, stores.at[i]) for i, (a, b) in enumerate(arrays)]
    for copy in load:
        copy.start()

    @pl.when(odd)
    def _():
        pl.semaphore_wait(barrier, 1)
        remote(f_hbm, other, fsend, frecv, (me, rep - 1)).start()
        signal(inside, me, rep - 1)

    load[0].wait()

    def pick(o, carry):
        for k in range(2):
            b = slot_ref[k, o]
            chunk = g_ref[jnp.maximum(b, 0)]
            pay[k, o] = jnp.where(b >= 0, chunk, 0.0)
        return carry

    lax.fori_loop(0, OWNERS, pick, 0, unroll=8)

    @pl.when(site)
    def _():
        pl.semaphore_wait(barrier, 45)
        pl.semaphore_wait(inside, 1)
        for s in range(1, 16):
            signal(stage2, z * 16 + wrap(yc + s, 16), rep)
        pl.semaphore_wait(stage2, 15)
        signal(go2, me, rep + 1)

    @pl.when(odd)
    def _():
        pl.semaphore_wait(go2, 1)

    def send(s, carry):
        d = lax.rem(me + s * 37, OWNERS)
        for k in range(2):
            remote(pay.at[k, d], gq.at[rep, me // 2, lax.rem(me, 2)], send1, recv1.at[rep], (d, 2 * k)).start()
        return carry

    lax.fori_loop(1, OWNERS, send, 0, unroll=4)
    for k in range(2):
        own_chunk = gq.at[rep, me // 2, lax.rem(me, 2)]

        @pl.when(rep != 2 * k)
        def _():
            remote(pay.at[k, me], own_chunk, send1, recv1.at[rep], (me, 2 * k)).start()

        @pl.when(rep == 2 * k)
        def _():
            pltpu.make_async_copy(pay.at[k, me], own_chunk, recv1.at[rep]).start()

    @pl.when(site)
    def _():
        for s in range(1, 8):
            signal(stage3, wrap(z + s, 8) * 16 + yc, rep)
        pl.semaphore_wait(stage3, 7)
        signal(stage4, me, twin)
        pl.semaphore_wait(stage4, 1)
        signal(go3, me, rep + 1)

    @pl.when(odd)
    def _():
        pl.semaphore_wait(go3, 1)

    load[1].wait()
    load[2].wait()
    grad = g_ref[...]
    new_m = MOMENT_DECAY * m_ref[...] + (1.0 - MOMENT_DECAY) * grad
    new_v = SECOND_DECAY * v_ref[...] + (1.0 - SECOND_DECAY) * grad * grad
    nm_ref[...] = new_m
    nv_ref[...] = new_v
    store[1].start()
    store[2].start()
    adam = new_m / (jnp.sqrt(new_v) + ADAM_EPSILON)
    rows = jnp.sum(adam * adam, axis=1)
    part[...] = jnp.zeros_like(part)
    part[0:BLOCKS, :] = rows
    total = lax.dot_general(
        jnp.ones((8, 128), f32), part[...], (((1,), (1,)), ((), ())),
        precision=lax.Precision.HIGHEST, preferred_element_type=f32,
    )[0:1]

    def z_peer(s):
        return wrap(z + s, 8) * 16 + yc

    def y_peer(s):
        return z * 16 + wrap(yc + s, 16)

    def share(buf, step, here, n, value, peer):
        buf[here] = value
        for s in range(1, n):
            remote(buf.at[here], buf.at[here], asend.at[step], arecv.at[step], (peer(s), rep)).start()

    def shared(buf, step, n):
        some = buf.at[pl.ds(0, n - 1)]
        pltpu.make_async_copy(some, some, asend.at[step]).wait()
        pltpu.make_async_copy(some, some, arecv.at[step]).wait()
        return functools.reduce(lambda x, y: x + y, [buf[s] for s in range(n)])

    share(ga, 0, yc, 16, total, y_peer)
    load[3].wait()

    def locate(b, carry):
        o = owner_ref[b]
        where_ref[b] = o + OWNERS * jnp.where(slot_ref[0, o] == b, 0, 1)
        return carry

    lax.fori_loop(0, BLOCKS, locate, 0, unroll=8)

    def share_z():
        share(gz, 1, z, 8, shared(ga, 0, 16), z_peer)

    def share_x():
        gx[rep] = shared(gz, 1, 8)

        @pl.when(odd)
        def _():
            for k in range(2):
                remote(gx.at[rep], gx.at[rep], asend.at[2], arecv.at[2], (me, 2 * k)).start()

        @pl.when(site)
        def _():
            remote(gx.at[rep], gx.at[rep], asend.at[3], arecv.at[2], (me, twin)).start()

    @pl.when(odd)
    def _():
        share_z()
        share_x()

    def units(n, sem):
        while n > 0:
            some = xq.at[0, pl.ds(0, min(n, 64))]
            pltpu.make_async_copy(some, some, sem).wait()
            n -= 64

    def group(dz):
        return pl.ds(wrap(z + dz, 8) * 8, 8)

    def each(dzs, act):
        for dz in dzs:
            base = wrap(z + dz, 8) * 16
            if dz == 0:
                act(me, True)

            def body(j, carry):
                act(base + wrap(yc + j, 16), False)
                return carry

            lax.fori_loop(1 if dz == 0 else 0, 16, body, 0, unroll=4 if dz else 3)

    @pl.when(site)
    def _():
        row = lax.broadcasted_iota(jnp.int32, (BLOCK, BLOCK), 0)
        col = lax.broadcasted_iota(jnp.int32, (BLOCK, BLOCK), 1)
        eye_ref[...] = jnp.where(row == col, 1.0, 0.0)
        for q in range(4):
            pltpu.make_async_copy(gq.at[q], gq.at[q], recv1.at[q]).wait()
        for q in range(4):
            both = jnp.concatenate([gq[q, :, 0], gq[q, :, 1]], axis=1)
            g_full[:, q * 128 : (q + 1) * 128] = both.reshape(BLOCK, 128)
        gs = split(g_full[...])
        gram[...] = mm(gs, gs, ((0,), (0,)))
        for i in range(4):
            panel = gram.at[pl.ds(128 * i, 128), pl.ds(128 * i, BLOCK - 128 * i)]
            there = other.at[pl.ds(128 * i, 128), pl.ds(128 * i, BLOCK - 128 * i)]
            remote(panel, there, usend.at[i], urecv.at[i], (me, rep + 1)).start()
        left_gram = mm(gs, gs, ((1,), (1,)))
        left = FACTOR_DECAY * f_ref[...] + (1.0 - FACTOR_DECAY) * left_gram
        nf_ref[...] = left
        store[3].start()
        share_z()
        left_root = run(root_steps(left, eye_ref[...]))
        applied = split(mm(left_root, gs))
        share_x()
        remote(f_hbm, other, fsend, frecv, (me, rep + 1)).wait_recv()
        right = FACTOR_DECAY * other[...] + (1.0 - FACTOR_DECAY) * gram[...]
        right_root = run(root_steps(right, eye_ref[...]))
        shampoo = mm(applied, right_root)
        remote(gx.at[rep], gx.at[rep], asend.at[3], arecv.at[2], (me, twin)).wait_send()
        pltpu.make_async_copy(gx.at[pl.ds(0, 3)], gx.at[pl.ds(0, 3)], arecv.at[2]).wait()
        sums[...] = gx[0] + gx[1] + gx[2] + gx[3]
        b = slot_ref[slot, me]
        lane = lax.broadcasted_iota(jnp.int32, sums.shape, 1)
        adam_total = jnp.sum(jnp.where(lane == b, sums[...], 0.0), keepdims=True)
        shampoo_total = jnp.sum(shampoo * shampoo, keepdims=True)
        scale = jnp.sqrt(adam_total) / jnp.sqrt(shampoo_total + NORM_EPSILON)
        for q in range(4):
            part_q = (shampoo[:, q * 128 : (q + 1) * 128] * scale).reshape(64, 8, 128)
            xq[q, :, 0] = part_q[:, 0:4]
            xq[q, :, 1] = part_q[:, 4:8]
        for phase, dzs in enumerate(PHASES):
            for dz in dzs:
                for c in (1, 3):
                    remote(xq.at[c, group(dz)], xs.at[slot, group(dz)], spsend, sprecv.at[slot, phase], (me, c)).start()

        def own(d, same):
            chunk = xq.at[rep, d // 2, lax.rem(d, 2)]
            if same:
                pltpu.make_async_copy(chunk, ret.at[OWNERS * slot + me], recv2).start()
            else:
                remote(chunk, ret.at[OWNERS * slot + me], send2, recv2, (d, rep)).start()

        def across(d, same):
            remote(xq.at[twin, d // 2, lax.rem(d, 2)], ret.at[OWNERS * slot + me], send2, recv2, (d, twin)).start()

        def aside(d, same):
            for c in (1, 3):
                remote(xq.at[c, d // 2, lax.rem(d, 2)], ret.at[OWNERS * slot + me], send2, recv2, (d, c)).start()

        def everyone(act):
            act(me, True)

            def body(s, carry):
                act(lax.rem(me + s * 37, OWNERS), False)
                return carry

            lax.fori_loop(1, OWNERS, body, 0, unroll=4)

        everyone(own)
        everyone(across)
        each(DIRECT, aside)
        units(RELAYED, spsend)
        units(127 + 16 * len(DIRECT), send2)
        one = pay.at[0, 0]
        pltpu.make_async_copy(one, one, send2).wait()

    @pl.when(odd)
    def _():
        for i in range(4):
            there = other.at[pl.ds(128 * i, 128), pl.ds(128 * i, BLOCK - 128 * i)]
            remote(there, there, usend.at[i], urecv.at[i], (me, rep - 1)).wait_recv()
        for i in range(4):
            for j in range(4):
                a, b = slice(128 * i, 128 * i + 128), slice(128 * j, 128 * j + 128)
                square = other[a, b] if i <= j else other[b, a].T
                nf_ref[a, b] = FACTOR_DECAY * f_ref[a, b] + (1.0 - FACTOR_DECAY) * square
        store[3].start()

        def give(d, same):
            for k in range(2):
                remote(xs.at[k, d // 2, lax.rem(d, 2)], ret.at[OWNERS * k + me], send2, recv2, (d, rep)).start()

        for phase, dzs in enumerate(PHASES):
            some = xs.at[0, pl.ds(0, 8 * len(dzs))]
            for k in range(2):
                pltpu.make_async_copy(some, some, sprecv.at[k, phase]).wait()
            each(dzs, give)
        units(RELAYED, send2)
        pair = gx.at[pl.ds(0, 2)]
        pltpu.make_async_copy(pair, pair, asend.at[2]).wait()
        remote(f_hbm, other, fsend, frecv, (me, rep - 1)).wait_send()

    pltpu.make_async_copy(pay.at[:, pl.ds(0, 127)], pay.at[:, pl.ds(0, 127)], send1).wait()
    for k in range(2):
        @pl.when(rep != 2 * k)
        def _():
            pltpu.make_async_copy(pay.at[k, 0], pay.at[k, 0], send1).wait()

    pltpu.make_async_copy(ret, ret, recv2).wait()

    def place(b, carry):
        dir_ref[b] = ret[where_ref[b]]
        return carry

    lax.fori_loop(0, BLOCKS, place, 0, unroll=8)
    store[0].start()

    @pl.when(site)
    def _():
        for i in range(4):
            panel = gram.at[pl.ds(128 * i, 128), pl.ds(128 * i, BLOCK - 128 * i)]
            remote(panel, panel, usend.at[i], urecv.at[i], (me, rep + 1)).wait_send()

    for copy in store:
        copy.wait()


def pass_on(*refs):
    sources, results, held, sems = refs[:4], refs[4:8], refs[8:12], refs[12]
    arriving, leaving = [], []
    for i in range(4):
        half = sources[i].shape[0] // 2
        for h in range(2):
            rows = pl.ds(h * half, half)
            arriving.append(pltpu.make_async_copy(sources[i].at[rows], held[i].at[rows], sems.at[2 * i + h, 0]))
            leaving.append(pltpu.make_async_copy(held[i].at[rows], results[i].at[rows], sems.at[2 * i + h, 1]))
    for copy in arriving:
        copy.start()
    for come, go in zip(arriving, leaving):
        come.wait()
        go.start()
    for copy in leaving:
        copy.wait()


def shards(gradients, moments, second_moments, factors, owner_of, slot_order):
    anywhere = pl.BlockSpec(memory_space=pl.ANY)
    blocks = pltpu.VMEM((BLOCKS, 4, 128), f32)
    chunks2 = pltpu.VMEM((2 * OWNERS, 4, 128), f32)
    smem = pl.BlockSpec(memory_space=pltpu.SMEM)
    part = jax.ShapeDtypeStruct(gradients.shape, f32)
    chunks = lambda n: pltpu.VMEM((n, OWNERS, 4, 128), f32)
    halves = lambda n: pltpu.VMEM((n, 64, 2, 4, 128), f32)
    square = pltpu.VMEM((BLOCK, BLOCK), f32)
    dma = pltpu.SemaphoreType.DMA
    regular = pltpu.SemaphoreType.REGULAR
    out_shape = (part, part, part, jax.ShapeDtypeStruct((BLOCK, BLOCK), f32))
    results = pl.pallas_call(
        kernel,
        out_shape=out_shape,
        in_specs=[smem, smem] + [anywhere] * 4,
        out_specs=(anywhere,) * 4,
        scratch_shapes=[
            blocks, blocks, blocks, square, blocks, blocks, blocks, square, pltpu.SMEM((BLOCKS,), jnp.int32),
            chunks(2), halves(4), square, square, halves(4), halves(2), chunks2, square, square,
            pltpu.VMEM((1, 256), f32), pltpu.VMEM((256, 128), f32),
            pltpu.VMEM((16, 1, 256), f32), pltpu.VMEM((8, 1, 256), f32), pltpu.VMEM((4, 1, 256), f32),
            regular, regular, regular, regular, regular, regular,
            dma, dma((4,)), dma, dma, dma((4,)), dma((4,)), dma, dma((2, 2)), dma, dma, dma((4,)), dma((3,)),
            dma((4,)), dma((4,)),
        ],
        compiler_params=pltpu.CompilerParams(
            collective_id=0, has_side_effects=True, vmem_limit_bytes=56 << 20
        ),
    )(slot_order.T, owner_of, gradients, moments, second_moments, factors.reshape(BLOCK, BLOCK))
    direction, new_m, new_v, new_f = pl.pallas_call(
        pass_on,
        out_shape=out_shape,
        in_specs=[anywhere] * 4,
        out_specs=(anywhere,) * 4,
        scratch_shapes=[blocks, blocks, blocks, square, dma((8, 2))],
    )(*results)
    return direction, new_m, new_v, new_f[None, None]


def solution(mesh):
    split_blocks = P(None, "fsdp", "rep")
    return jax.shard_map(
        shards,
        mesh=mesh,
        in_specs=(split_blocks, split_blocks, split_blocks, P("fsdp", "rep", None, None), P(), P()),
        out_specs=(split_blocks, split_blocks, split_blocks, P("fsdp", "rep", None, None)),
        check_vma=False,
    )
```

```python
import functools

import jax
import jax.numpy as jnp
from jax import lax
from jax.experimental import pallas as pl
from jax.experimental.pallas import tpu as pltpu
from jax.sharding import PartitionSpec as P

MOMENT_DECAY = 0.9
SECOND_DECAY = 0.95
FACTOR_DECAY = 0.95
DAMPING = 0.1
ADAM_EPSILON = 1e-08
NORM_EPSILON = 1e-06

BLOCK = 512
OWNERS = 128
BLOCKS = 192
MESH = pl.DeviceIdType.MESH
DIRECT = (0, 4)
EARLY = 320
PHASES = ((1, 2, 3), (5, 6, 7))
RELAYED = 16 * sum(len(p) for p in PHASES)
f32 = jnp.float32
bf16 = jnp.bfloat16


def split(x):
    hi = x.astype(bf16)
    return hi, (x - hi.astype(f32)).astype(bf16)


def mm(a, b, dims=((1,), (0,))):
    (ah, al), (bh, bl) = a, b

    def dot(x, y):
        return lax.dot_general(x, y, (dims, ((), ())), preferred_element_type=f32)

    return dot(ah, bh) + (dot(ah, bl) + dot(al, bh))


def damp(factor, eye):
    damped = factor + DAMPING * eye
    frobenius = jnp.sqrt(jnp.sum(damped * damped, keepdims=True) + NORM_EPSILON)
    return damped * (1.0 / frobenius), frobenius


def root_steps(factor, eye):
    m, c = damp(factor, eye)
    ms = split(m)
    n = mm(ms, ms)
    q = split(1.5625 * eye - 0.625 * m + 0.0625 * n)
    yield
    q = split(mm(q, q))
    yield
    m1 = mm(q, ms)
    m1s = split(m1)
    yield
    n1 = mm(m1s, m1s)
    p = split(1.5625 * eye - 0.625 * m1 + 0.0625 * n1)
    w = split(1.25 * m1 - 0.25 * n1)
    yield
    p = split(mm(p, p))
    yield
    y = mm(p, w)
    u = split(1.5625 * eye - 0.3125 * m1 - 0.25 * y)
    t0 = split((1.25 * eye - 0.25 * m) * lax.rsqrt(jnp.sqrt(c)))
    yield
    yield split(mm(t0, u))


def run(gen):
    last = None
    for last in gen:
        pass
    return last


def remote(src, dst, send, recv, device):
    return pltpu.make_async_remote_copy(
        src_ref=src, dst_ref=dst, send_sem=send, recv_sem=recv, device_id=device, device_id_type=MESH
    )


def wrap(v, n):
    return jnp.where(v >= n, v - n, v)


def kernel(
    slot_ref, owner_ref, g_hbm, m_hbm, v_hbm, f_hbm,
    dir_hbm, nm_hbm, nv_hbm, nf_hbm,
    g_ref, m_ref, v_ref, f_ref, dir_ref, nm_ref, nv_ref, nf_ref, where_ref,
    pay, gq, other, gram, xq, xs, ret, eye_ref, g_full, sums, part, ga, gz, gx,
    inside, more, stage2, stage3, stage4, go2, go3,
    send1, recv1, fsend, frecv, usend, urecv, spsend, sprecv, send2, recv2, asend, arecv, loads, stores,
):
    me = lax.axis_index("fsdp")
    rep = lax.axis_index("rep")
    z = me // 16
    yc = me - z * 16
    chip = me // 2
    core = me - 2 * chip
    y = chip - 8 * z
    site = lax.rem(rep, 2) == 0
    odd = jnp.logical_not(site)
    slot = rep // 2
    twin = wrap(rep + 2, 4)

    barrier = pltpu.get_barrier_semaphore()

    def signal(sem, d, r):
        pl.semaphore_signal(sem, inc=1, device_id=(d, r), device_id_type=MESH)

    @pl.when(site)
    def _():
        signal(barrier, me, rep + 1)
        for t in range(2):
            for s in range(0 if t else 1, 16):
                signal(barrier, z * 16 + wrap(yc + s, 16), wrap(rep + 2 * t, 4))
            for s in range(1, 8):
                signal(barrier, wrap(z + s, 8) * 16 + yc, wrap(rep + 2 * t, 4))

    arrays = ((g_hbm, g_ref), (m_hbm, m_ref), (v_hbm, v_ref), (f_hbm, f_ref))
    load = [pltpu.make_async_copy(a, b, loads.at[i]) for i, (a, b) in enumerate(arrays)]
    arrays = ((dir_ref, dir_hbm), (nm_ref, nm_hbm), (nv_ref, nv_hbm), (nf_ref, nf_hbm))
    store = [pltpu.make_async_copy(a, b, stores.at[i]) for i, (a, b) in enumerate(arrays)]
    for copy in load:
        copy.start()

    def factor(part, there):
        rows = pl.ds(0, EARLY) if part == 0 else pl.ds(EARLY, BLOCK - EARLY)
        return remote(f_hbm.at[rows], other.at[rows], fsend.at[part], frecv.at[part], (me, there))

    @pl.when(odd)
    def _():
        pl.semaphore_wait(barrier, 1)
        factor(0, rep - 1).start()
        signal(inside, me, rep - 1)

    load[0].wait()

    def pick(o, carry):
        for k in range(2):
            b = slot_ref[k, o]
            chunk = g_ref[jnp.maximum(b, 0)]
            pay[k, o] = jnp.where(b >= 0, chunk, 0.0)
        return carry

    lax.fori_loop(0, OWNERS, pick, 0, unroll=8)

    @pl.when(site)
    def _():
        pl.semaphore_wait(barrier, 45)
        pl.semaphore_wait(inside, 1)
        for s in range(1, 16):
            signal(stage2, z * 16 + wrap(yc + s, 16), rep)
        pl.semaphore_wait(stage2, 15)
        signal(go2, me, rep + 1)

    @pl.when(odd)
    def _():
        pl.semaphore_wait(go2, 1)

    own_chunk = gq.at[rep, chip, core]

    def send(s, d):
        d = wrap(d + 37, OWNERS)
        for k in range(2):
            remote(pay.at[k, d], own_chunk, send1, recv1.at[rep], (d, 2 * k)).start()
        return d

    lax.fori_loop(1, OWNERS, send, me, unroll=4)
    for k in range(2):

        @pl.when(rep != 2 * k)
        def _():
            remote(pay.at[k, me], own_chunk, send1, recv1.at[rep], (me, 2 * k)).start()

        @pl.when(rep == 2 * k)
        def _():
            pltpu.make_async_copy(pay.at[k, me], own_chunk, recv1.at[rep]).start()

    @pl.when(site)
    def _():
        for s in range(1, 8):
            signal(stage3, wrap(z + s, 8) * 16 + yc, rep)
        pl.semaphore_wait(stage3, 7)
        signal(stage4, me, twin)
        pl.semaphore_wait(stage4, 1)
        signal(go3, me, rep + 1)

    @pl.when(odd)
    def _():
        pl.semaphore_wait(go3, 1)

    load[1].wait()
    load[2].wait()
    grad = g_ref[...]
    new_m = MOMENT_DECAY * m_ref[...] + (1.0 - MOMENT_DECAY) * grad
    new_v = SECOND_DECAY * v_ref[...] + (1.0 - SECOND_DECAY) * grad * grad
    nm_ref[...] = new_m
    nv_ref[...] = new_v
    store[1].start()
    store[2].start()
    adam = new_m / (jnp.sqrt(new_v) + ADAM_EPSILON)
    rows = jnp.sum(adam * adam, axis=1)
    part[...] = jnp.zeros_like(part)
    part[0:BLOCKS, :] = rows
    total = lax.dot_general(
        jnp.ones((8, 128), f32), part[...], (((1,), (1,)), ((), ())),
        precision=lax.Precision.HIGHEST, preferred_element_type=f32,
    )[0:1]

    def z_peer(s):
        return wrap(z + s, 8) * 16 + yc

    def y_peer(s):
        return z * 16 + wrap(yc + s, 16)

    def share(buf, step, here, n, value, peer):
        buf[here] = value
        for s in range(1, n):
            remote(buf.at[here], buf.at[here], asend.at[step], arecv.at[step], (peer(s), rep)).start()

    def shared(buf, step, n):
        some = buf.at[pl.ds(0, n - 1)]
        pltpu.make_async_copy(some, some, asend.at[step]).wait()
        pltpu.make_async_copy(some, some, arecv.at[step]).wait()
        return functools.reduce(lambda x, y: x + y, [buf[s] for s in range(n)])

    share(ga, 0, yc, 16, total, y_peer)
    load[3].wait()

    def locate(b, carry):
        o = owner_ref[b]
        where_ref[b] = o + OWNERS * jnp.where(slot_ref[0, o] == b, 0, 1)
        return carry

    lax.fori_loop(0, BLOCKS, locate, 0, unroll=8)

    def share_z():
        share(gz, 1, z, 8, shared(ga, 0, 16), z_peer)

    def share_x():
        gx[rep] = shared(gz, 1, 8)

        @pl.when(odd)
        def _():
            for k in range(2):
                remote(gx.at[rep], gx.at[rep], asend.at[2], arecv.at[2], (me, 2 * k)).start()

        @pl.when(site)
        def _():
            remote(gx.at[rep], gx.at[rep], asend.at[3], arecv.at[2], (me, twin)).start()

    @pl.when(odd)
    def _():
        share_z()
        share_x()

    def units(n, sem):
        while n > 0:
            some = xq.at[0, pl.ds(0, min(n, 64))]
            pltpu.make_async_copy(some, some, sem).wait()
            n -= 64

    def group(dz):
        return pl.ds(wrap(z + dz, 8) * 8, 8)

    def each(dzs, act):
        for dz in dzs:
            base = wrap(z + dz, 8) * 8
            if dz == 0:
                act(chip, core, True)
                act(chip, 1 - core, False)

            def body(j, carry):
                for c in range(2):
                    act(base + wrap(y + j, 8), c, False)
                return carry

            lax.fori_loop(0 if dz else 1, 8, body, 0, unroll=4 if dz else 7)

    def everyone(act):
        act(chip, core, True)
        act(chip, 1 - core, False)

        def body(s, e):
            e = wrap(e + 37, 64)
            for c in range(2):
                act(e, c, False)
            return e

        lax.fori_loop(1, 64, body, chip, unroll=3)

    @pl.when(site)
    def _():
        row = lax.broadcasted_iota(jnp.int32, (BLOCK, BLOCK), 0)
        col = lax.broadcasted_iota(jnp.int32, (BLOCK, BLOCK), 1)
        eye_ref[...] = jnp.where(row == col, 1.0, 0.0)
        for q in range(4):
            pltpu.make_async_copy(gq.at[q], gq.at[q], recv1.at[q]).wait()
        signal(more, me, rep + 1)
        for q in range(4):
            both = jnp.concatenate([gq[q, :, 0], gq[q, :, 1]], axis=1)
            g_full[:, q * 128 : (q + 1) * 128] = both.reshape(BLOCK, 128)
        gs = split(g_full[...])
        gram[...] = mm(gs, gs, ((0,), (0,)))
        for i in range(4):
            panel = gram.at[pl.ds(128 * i, 128), pl.ds(128 * i, BLOCK - 128 * i)]
            there = other.at[pl.ds(128 * i, 128), pl.ds(128 * i, BLOCK - 128 * i)]
            remote(panel, there, usend.at[i], urecv.at[i], (me, rep + 1)).start()
        left_gram = mm(gs, gs, ((1,), (1,)))
        left = FACTOR_DECAY * f_ref[...] + (1.0 - FACTOR_DECAY) * left_gram
        nf_ref[...] = left
        store[3].start()
        share_z()
        left_root = run(root_steps(left, eye_ref[...]))
        applied = split(mm(left_root, gs))
        share_x()
        factor(0, rep + 1).wait_recv()
        factor(1, rep + 1).wait_recv()
        right = FACTOR_DECAY * other[...] + (1.0 - FACTOR_DECAY) * gram[...]
        right_root = run(root_steps(right, eye_ref[...]))
        shampoo = mm(applied, right_root)
        remote(gx.at[rep], gx.at[rep], asend.at[3], arecv.at[2], (me, twin)).wait_send()
        pltpu.make_async_copy(gx.at[pl.ds(0, 3)], gx.at[pl.ds(0, 3)], arecv.at[2]).wait()
        sums[...] = gx[0] + gx[1] + gx[2] + gx[3]
        b = slot_ref[slot, me]
        lane = lax.broadcasted_iota(jnp.int32, sums.shape, 1)
        adam_total = jnp.sum(jnp.where(lane == b, sums[...], 0.0), keepdims=True)
        shampoo_total = jnp.sum(shampoo * shampoo, keepdims=True)
        scale = jnp.sqrt(adam_total) / jnp.sqrt(shampoo_total + NORM_EPSILON)
        for q in range(4):
            part_q = (shampoo[:, q * 128 : (q + 1) * 128] * scale).reshape(64, 8, 128)
            xq[q, :, 0] = part_q[:, 0:4]
            xq[q, :, 1] = part_q[:, 4:8]
        for phase, dzs in enumerate(PHASES):
            for dz in dzs:
                for c in (1, 3):
                    remote(xq.at[c, group(dz)], xs.at[slot, group(dz)], spsend, sprecv.at[slot, phase], (me, c)).start()

        place_there = ret.at[OWNERS * slot + me]

        def own(e, c, same):
            if same:
                pltpu.make_async_copy(xq.at[rep, e, c], place_there, recv2).start()
            else:
                remote(xq.at[rep, e, c], place_there, send2, recv2, (2 * e + c, rep)).start()

        def across(e, c, same):
            remote(xq.at[twin, e, c], place_there, send2, recv2, (2 * e + c, twin)).start()

        def aside(e, c, same):
            for q in (1, 3):
                remote(xq.at[q, e, c], place_there, send2, recv2, (2 * e + c, q)).start()

        everyone(own)
        everyone(across)
        each(DIRECT, aside)
        units(RELAYED, spsend)
        units(127 + 16 * len(DIRECT), send2)
        one = pay.at[0, 0]
        pltpu.make_async_copy(one, one, send2).wait()

    @pl.when(odd)
    def _():
        pl.semaphore_wait(more, 1)
        factor(1, rep - 1).start()
        for i in range(4):
            there = other.at[pl.ds(128 * i, 128), pl.ds(128 * i, BLOCK - 128 * i)]
            remote(there, there, usend.at[i], urecv.at[i], (me, rep - 1)).wait_recv()
        for i in range(4):
            for j in range(4):
                a, b = slice(128 * i, 128 * i + 128), slice(128 * j, 128 * j + 128)
                square = other[a, b] if i <= j else other[b, a].T
                nf_ref[a, b] = FACTOR_DECAY * f_ref[a, b] + (1.0 - FACTOR_DECAY) * square
        store[3].start()

        def give(e, c, same):
            for k in range(2):
                remote(xs.at[k, e, c], ret.at[OWNERS * k + me], send2, recv2, (2 * e + c, rep)).start()

        for phase, dzs in enumerate(PHASES):
            some = xs.at[0, pl.ds(0, 8 * len(dzs))]
            for k in range(2):
                pltpu.make_async_copy(some, some, sprecv.at[k, phase]).wait()
            each(dzs, give)
        units(RELAYED, send2)
        pair = gx.at[pl.ds(0, 2)]
        pltpu.make_async_copy(pair, pair, asend.at[2]).wait()
        factor(0, rep - 1).wait_send()
        factor(1, rep - 1).wait_send()

    pltpu.make_async_copy(pay.at[:, pl.ds(0, 127)], pay.at[:, pl.ds(0, 127)], send1).wait()
    for k in range(2):
        @pl.when(rep != 2 * k)
        def _():
            pltpu.make_async_copy(pay.at[k, 0], pay.at[k, 0], send1).wait()

    pltpu.make_async_copy(ret, ret, recv2).wait()

    def place(b, carry):
        dir_ref[b] = ret[where_ref[b]]
        return carry

    lax.fori_loop(0, BLOCKS, place, 0, unroll=8)
    store[0].start()

    @pl.when(site)
    def _():
        for i in range(4):
            panel = gram.at[pl.ds(128 * i, 128), pl.ds(128 * i, BLOCK - 128 * i)]
            remote(panel, panel, usend.at[i], urecv.at[i], (me, rep + 1)).wait_send()

    for copy in store:
        copy.wait()


def pass_on(*refs):
    sources, results, held, sems = refs[:4], refs[4:8], refs[8:12], refs[12]
    arriving, leaving = [], []
    for i in range(4):
        half = sources[i].shape[0] // 2
        for h in range(2):
            rows = pl.ds(h * half, half)
            arriving.append(pltpu.make_async_copy(sources[i].at[rows], held[i].at[rows], sems.at[2 * i + h, 0]))
            leaving.append(pltpu.make_async_copy(held[i].at[rows], results[i].at[rows], sems.at[2 * i + h, 1]))
    for copy in arriving:
        copy.start()
    for come, go in zip(arriving, leaving):
        come.wait()
        go.start()
    for copy in leaving:
        copy.wait()


def shards(gradients, moments, second_moments, factors, owner_of, slot_order):
    anywhere = pl.BlockSpec(memory_space=pl.ANY)
    blocks = pltpu.VMEM((BLOCKS, 4, 128), f32)
    chunks2 = pltpu.VMEM((2 * OWNERS, 4, 128), f32)
    smem = pl.BlockSpec(memory_space=pltpu.SMEM)
    part = jax.ShapeDtypeStruct(gradients.shape, f32)
    chunks = lambda n: pltpu.VMEM((n, OWNERS, 4, 128), f32)
    halves = lambda n: pltpu.VMEM((n, 64, 2, 4, 128), f32)
    square = pltpu.VMEM((BLOCK, BLOCK), f32)
    dma = pltpu.SemaphoreType.DMA
    regular = pltpu.SemaphoreType.REGULAR
    out_shape = (part, part, part, jax.ShapeDtypeStruct((BLOCK, BLOCK), f32))
    results = pl.pallas_call(
        kernel,
        out_shape=out_shape,
        in_specs=[smem, smem] + [anywhere] * 4,
        out_specs=(anywhere,) * 4,
        scratch_shapes=[
            blocks, blocks, blocks, square, blocks, blocks, blocks, square, pltpu.SMEM((BLOCKS,), jnp.int32),
            chunks(2), halves(4), square, square, halves(4), halves(2), chunks2, square, square,
            pltpu.VMEM((1, 256), f32), pltpu.VMEM((256, 128), f32),
            pltpu.VMEM((16, 1, 256), f32), pltpu.VMEM((8, 1, 256), f32), pltpu.VMEM((4, 1, 256), f32),
            regular, regular, regular, regular, regular, regular, regular,
            dma, dma((4,)), dma((2,)), dma((2,)), dma((4,)), dma((4,)), dma, dma((2, 2)), dma, dma, dma((4,)), dma((3,)),
            dma((4,)), dma((4,)),
        ],
        compiler_params=pltpu.CompilerParams(
            collective_id=0, has_side_effects=True, vmem_limit_bytes=56 << 20
        ),
    )(slot_order.T, owner_of, gradients, moments, second_moments, factors.reshape(BLOCK, BLOCK))
    direction, new_m, new_v, new_f = pl.pallas_call(
        pass_on,
        out_shape=out_shape,
        in_specs=[anywhere] * 4,
        out_specs=(anywhere,) * 4,
        scratch_shapes=[blocks, blocks, blocks, square, dma((8, 2))],
    )(*results)
    return direction, new_m, new_v, new_f[None, None]


def solution(mesh):
    split_blocks = P(None, "fsdp", "rep")
    return jax.shard_map(
        shards,
        mesh=mesh,
        in_specs=(split_blocks, split_blocks, split_blocks, P("fsdp", "rep", None, None), P(), P()),
        out_specs=(split_blocks, split_blocks, split_blocks, P("fsdp", "rep", None, None)),
        check_vma=False,
    )
```

```python
import functools

import jax
import jax.numpy as jnp
from jax import lax
from jax.experimental import pallas as pl
from jax.experimental.pallas import tpu as pltpu
from jax.sharding import PartitionSpec as P

MOMENT_DECAY = 0.9
SECOND_DECAY = 0.95
FACTOR_DECAY = 0.95
DAMPING = 0.1
ADAM_EPSILON = 1e-08
NORM_EPSILON = 1e-06

BLOCK = 512
OWNERS = 128
BLOCKS = 192
MESH = pl.DeviceIdType.MESH
DIRECT = (0, 4)
EARLY = 256
PHASES = ((1, 2, 3), (5, 6, 7))
RELAYED = 16 * sum(len(p) for p in PHASES)
f32 = jnp.float32
bf16 = jnp.bfloat16


def split(x):
    hi = x.astype(bf16)
    return hi, (x - hi.astype(f32)).astype(bf16)


def mm(a, b, dims=((1,), (0,))):
    (ah, al), (bh, bl) = a, b

    def dot(x, y):
        return lax.dot_general(x, y, (dims, ((), ())), preferred_element_type=f32)

    return dot(ah, bh) + (dot(ah, bl) + dot(al, bh))


def damp(factor, eye):
    damped = factor + DAMPING * eye
    frobenius = jnp.sqrt(jnp.sum(damped * damped, keepdims=True) + NORM_EPSILON)
    return damped * (1.0 / frobenius), frobenius


def root_steps(factor, eye):
    m, c = damp(factor, eye)
    ms = split(m)
    n = mm(ms, ms)
    q = split(1.5625 * eye - 0.625 * m + 0.0625 * n)
    yield
    q = split(mm(q, q))
    yield
    m1 = mm(q, ms)
    m1s = split(m1)
    yield
    n1 = mm(m1s, m1s)
    p = split(1.5625 * eye - 0.625 * m1 + 0.0625 * n1)
    w = split(1.25 * m1 - 0.25 * n1)
    yield
    p = split(mm(p, p))
    yield
    y = mm(p, w)
    u = split(1.5625 * eye - 0.3125 * m1 - 0.25 * y)
    t0 = split((1.25 * eye - 0.25 * m) * lax.rsqrt(jnp.sqrt(c)))
    yield
    yield split(mm(t0, u))


def run(gen):
    last = None
    for last in gen:
        pass
    return last


def remote(src, dst, send, recv, device):
    return pltpu.make_async_remote_copy(
        src_ref=src, dst_ref=dst, send_sem=send, recv_sem=recv, device_id=device, device_id_type=MESH
    )


def wrap(v, n):
    return jnp.where(v >= n, v - n, v)


def kernel(
    slot_ref, owner_ref, g_hbm, m_hbm, v_hbm, f_hbm,
    dir_hbm, nm_hbm, nv_hbm, nf_hbm,
    g_ref, m_ref, v_ref, f_ref, dir_ref, nm_ref, nv_ref, nf_ref, where_ref,
    pay, gq, other, gram, xq, xs, ret, eye_ref, g_full, sums, part, ga, gz, gx,
    inside, more, stage2, stage3, stage4, go2, go3,
    send1, recv1, fsend, frecv, usend, urecv, spsend, sprecv, send2, recv2, asend, arecv, loads, stores,
):
    me = lax.axis_index("fsdp")
    rep = lax.axis_index("rep")
    z = me // 16
    yc = me - z * 16
    chip = me // 2
    core = me - 2 * chip
    y = chip - 8 * z
    site = lax.rem(rep, 2) == 0
    odd = jnp.logical_not(site)
    slot = rep // 2
    twin = wrap(rep + 2, 4)

    barrier = pltpu.get_barrier_semaphore()

    def signal(sem, d, r):
        pl.semaphore_signal(sem, inc=1, device_id=(d, r), device_id_type=MESH)

    @pl.when(site)
    def _():
        signal(barrier, me, rep + 1)
        for t in range(2):
            for s in range(0 if t else 1, 16):
                signal(barrier, z * 16 + wrap(yc + s, 16), wrap(rep + 2 * t, 4))
            for s in range(1, 8):
                signal(barrier, wrap(z + s, 8) * 16 + yc, wrap(rep + 2 * t, 4))

    arrays = ((g_hbm, g_ref), (m_hbm, m_ref), (v_hbm, v_ref), (f_hbm, f_ref))
    load = [pltpu.make_async_copy(a, b, loads.at[i]) for i, (a, b) in enumerate(arrays)]
    arrays = ((dir_ref, dir_hbm), (nm_ref, nm_hbm), (nv_ref, nv_hbm), (nf_ref, nf_hbm))
    store = [pltpu.make_async_copy(a, b, stores.at[i]) for i, (a, b) in enumerate(arrays)]
    for copy in load:
        copy.start()

    def factor(part, there):
        rows = pl.ds(0, EARLY) if part == 0 else pl.ds(EARLY, BLOCK - EARLY)
        return remote(f_hbm.at[rows], other.at[rows], fsend.at[part], frecv.at[part], (me, there))

    @pl.when(odd)
    def _():
        pl.semaphore_wait(barrier, 1)
        factor(0, rep - 1).start()
        signal(inside, me, rep - 1)

    load[0].wait()

    def pick(o, carry):
        for k in range(2):
            b = slot_ref[k, o]
            chunk = g_ref[jnp.maximum(b, 0)]
            pay[k, o] = jnp.where(b >= 0, chunk, 0.0)
        return carry

    lax.fori_loop(0, OWNERS, pick, 0, unroll=8)

    @pl.when(site)
    def _():
        pl.semaphore_wait(barrier, 45)
        pl.semaphore_wait(inside, 1)
        for s in range(1, 16):
            signal(stage2, z * 16 + wrap(yc + s, 16), rep)
        pl.semaphore_wait(stage2, 15)
        signal(go2, me, rep + 1)

    @pl.when(odd)
    def _():
        pl.semaphore_wait(go2, 1)

    own_chunk = gq.at[rep, chip, core]

    def send(s, d):
        d = wrap(d + 37, OWNERS)
        for k in range(2):
            remote(pay.at[k, d], own_chunk, send1, recv1.at[rep], (d, 2 * k)).start()
        return d

    lax.fori_loop(1, OWNERS, send, me, unroll=4)
    for k in range(2):

        @pl.when(rep != 2 * k)
        def _():
            remote(pay.at[k, me], own_chunk, send1, recv1.at[rep], (me, 2 * k)).start()

        @pl.when(rep == 2 * k)
        def _():
            pltpu.make_async_copy(pay.at[k, me], own_chunk, recv1.at[rep]).start()

    @pl.when(site)
    def _():
        for s in range(1, 8):
            signal(stage3, wrap(z + s, 8) * 16 + yc, rep)
        pl.semaphore_wait(stage3, 7)
        signal(stage4, me, twin)
        pl.semaphore_wait(stage4, 1)
        signal(go3, me, rep + 1)

    @pl.when(odd)
    def _():
        pl.semaphore_wait(go3, 1)

    load[1].wait()
    load[2].wait()
    grad = g_ref[...]
    new_m = MOMENT_DECAY * m_ref[...] + (1.0 - MOMENT_DECAY) * grad
    new_v = SECOND_DECAY * v_ref[...] + (1.0 - SECOND_DECAY) * grad * grad
    nm_ref[...] = new_m
    nv_ref[...] = new_v
    store[1].start()
    store[2].start()
    adam = new_m / (jnp.sqrt(new_v) + ADAM_EPSILON)
    rows = jnp.sum(adam * adam, axis=1)
    part[...] = jnp.zeros_like(part)
    part[0:BLOCKS, :] = rows
    total = lax.dot_general(
        jnp.ones((8, 128), f32), part[...], (((1,), (1,)), ((), ())),
        precision=lax.Precision.HIGHEST, preferred_element_type=f32,
    )[0:1]

    def z_peer(s):
        return wrap(z + s, 8) * 16 + yc

    def y_peer(s):
        return z * 16 + wrap(yc + s, 16)

    def share(buf, step, here, n, value, peer):
        buf[here] = value
        for s in range(1, n):
            remote(buf.at[here], buf.at[here], asend.at[step], arecv.at[step], (peer(s), rep)).start()

    def shared(buf, step, n):
        some = buf.at[pl.ds(0, n - 1)]
        pltpu.make_async_copy(some, some, asend.at[step]).wait()
        pltpu.make_async_copy(some, some, arecv.at[step]).wait()
        return functools.reduce(lambda x, y: x + y, [buf[s] for s in range(n)])

    share(ga, 0, yc, 16, total, y_peer)
    load[3].wait()

    def locate(b, carry):
        o = owner_ref[b]
        where_ref[b] = o + OWNERS * jnp.where(slot_ref[0, o] == b, 0, 1)
        return carry

    lax.fori_loop(0, BLOCKS, locate, 0, unroll=8)

    def share_z():
        share(gz, 1, z, 8, shared(ga, 0, 16), z_peer)

    def share_x():
        gx[rep] = shared(gz, 1, 8)

        @pl.when(odd)
        def _():
            for k in range(2):
                remote(gx.at[rep], gx.at[rep], asend.at[2], arecv.at[2], (me, 2 * k)).start()

        @pl.when(site)
        def _():
            remote(gx.at[rep], gx.at[rep], asend.at[3], arecv.at[2], (me, twin)).start()

    @pl.when(odd)
    def _():
        share_z()
        share_x()

    def units(n, sem):
        while n > 0:
            some = xq.at[0, pl.ds(0, min(n, 64))]
            pltpu.make_async_copy(some, some, sem).wait()
            n -= 64

    def group(dz):
        return pl.ds(wrap(z + dz, 8) * 8, 8)

    def each(dzs, act):
        for dz in dzs:
            base = wrap(z + dz, 8) * 8
            if dz == 0:
                act(chip, core, True)
                act(chip, 1 - core, False)

            def body(j, carry):
                for c in range(2):
                    act(base + wrap(y + j, 8), c, False)
                return carry

            lax.fori_loop(0 if dz else 1, 8, body, 0, unroll=4 if dz else 7)

    def everyone(act):
        act(chip, core, True)
        act(chip, 1 - core, False)

        def body(s, e):
            e = wrap(e + 37, 64)
            for c in range(2):
                act(e, c, False)
            return e

        lax.fori_loop(1, 64, body, chip, unroll=3)

    @pl.when(site)
    def _():
        row = lax.broadcasted_iota(jnp.int32, (BLOCK, BLOCK), 0)
        col = lax.broadcasted_iota(jnp.int32, (BLOCK, BLOCK), 1)
        eye_ref[...] = jnp.where(row == col, 1.0, 0.0)
        for q in range(4):
            pltpu.make_async_copy(gq.at[q], gq.at[q], recv1.at[q]).wait()
        signal(more, me, rep + 1)
        for q in range(4):
            both = jnp.concatenate([gq[q, :, 0], gq[q, :, 1]], axis=1)
            g_full[:, q * 128 : (q + 1) * 128] = both.reshape(BLOCK, 128)
        gs = split(g_full[...])
        gram[...] = mm(gs, gs, ((0,), (0,)))
        for i in range(4):
            panel = gram.at[pl.ds(128 * i, 128), pl.ds(128 * i, BLOCK - 128 * i)]
            there = other.at[pl.ds(128 * i, 128), pl.ds(128 * i, BLOCK - 128 * i)]
            remote(panel, there, usend.at[i], urecv.at[i], (me, rep + 1)).start()
        left_gram = mm(gs, gs, ((1,), (1,)))
        left = FACTOR_DECAY * f_ref[...] + (1.0 - FACTOR_DECAY) * left_gram
        nf_ref[...] = left
        store[3].start()
        share_z()
        left_root = run(root_steps(left, eye_ref[...]))
        applied = split(mm(left_root, gs))
        share_x()
        factor(0, rep + 1).wait_recv()
        factor(1, rep + 1).wait_recv()
        right = FACTOR_DECAY * other[...] + (1.0 - FACTOR_DECAY) * gram[...]
        right_root = run(root_steps(right, eye_ref[...]))
        shampoo = mm(applied, right_root)
        remote(gx.at[rep], gx.at[rep], asend.at[3], arecv.at[2], (me, twin)).wait_send()
        pltpu.make_async_copy(gx.at[pl.ds(0, 3)], gx.at[pl.ds(0, 3)], arecv.at[2]).wait()
        sums[...] = gx[0] + gx[1] + gx[2] + gx[3]
        b = slot_ref[slot, me]
        lane = lax.broadcasted_iota(jnp.int32, sums.shape, 1)
        adam_total = jnp.sum(jnp.where(lane == b, sums[...], 0.0), keepdims=True)
        shampoo_total = jnp.sum(shampoo * shampoo, keepdims=True)
        scale = jnp.sqrt(adam_total) / jnp.sqrt(shampoo_total + NORM_EPSILON)
        for q in range(4):
            part_q = (shampoo[:, q * 128 : (q + 1) * 128] * scale).reshape(64, 8, 128)
            xq[q, :, 0] = part_q[:, 0:4]
            xq[q, :, 1] = part_q[:, 4:8]
        for phase, dzs in enumerate(PHASES):
            for dz in dzs:
                for c in (1, 3):
                    remote(xq.at[c, group(dz)], xs.at[slot, group(dz)], spsend, sprecv.at[slot, phase], (me, c)).start()

        place_there = ret.at[OWNERS * slot + me]

        def own(e, c, same):
            if same:
                pltpu.make_async_copy(xq.at[rep, e, c], place_there, recv2).start()
            else:
                remote(xq.at[rep, e, c], place_there, send2, recv2, (2 * e + c, rep)).start()

        def across(e, c, same):
            remote(xq.at[twin, e, c], place_there, send2, recv2, (2 * e + c, twin)).start()

        def aside(e, c, same):
            for q in (1, 3):
                remote(xq.at[q, e, c], place_there, send2, recv2, (2 * e + c, q)).start()

        everyone(own)
        everyone(across)
        each(DIRECT, aside)
        units(RELAYED, spsend)
        units(127 + 16 * len(DIRECT), send2)
        one = pay.at[0, 0]
        pltpu.make_async_copy(one, one, send2).wait()

    @pl.when(odd)
    def _():
        pl.semaphore_wait(more, 1)
        factor(1, rep - 1).start()
        for i in range(4):
            there = other.at[pl.ds(128 * i, 128), pl.ds(128 * i, BLOCK - 128 * i)]
            remote(there, there, usend.at[i], urecv.at[i], (me, rep - 1)).wait_recv()
        for i in range(4):
            for j in range(4):
                a, b = slice(128 * i, 128 * i + 128), slice(128 * j, 128 * j + 128)
                square = other[a, b] if i <= j else other[b, a].T
                nf_ref[a, b] = FACTOR_DECAY * f_ref[a, b] + (1.0 - FACTOR_DECAY) * square
        store[3].start()

        def give(e, c, same):
            for k in range(2):
                remote(xs.at[k, e, c], ret.at[OWNERS * k + me], send2, recv2, (2 * e + c, rep)).start()

        for phase, dzs in enumerate(PHASES):
            some = xs.at[0, pl.ds(0, 8 * len(dzs))]
            for k in range(2):
                pltpu.make_async_copy(some, some, sprecv.at[k, phase]).wait()
            each(dzs, give)
        units(RELAYED, send2)
        pair = gx.at[pl.ds(0, 2)]
        pltpu.make_async_copy(pair, pair, asend.at[2]).wait()
        factor(0, rep - 1).wait_send()
        factor(1, rep - 1).wait_send()

    pltpu.make_async_copy(pay.at[:, pl.ds(0, 127)], pay.at[:, pl.ds(0, 127)], send1).wait()
    for k in range(2):
        @pl.when(rep != 2 * k)
        def _():
            pltpu.make_async_copy(pay.at[k, 0], pay.at[k, 0], send1).wait()

    pltpu.make_async_copy(ret, ret, recv2).wait()

    def place(b, carry):
        dir_ref[b] = ret[where_ref[b]]
        return carry

    lax.fori_loop(0, BLOCKS, place, 0, unroll=8)
    store[0].start()

    @pl.when(site)
    def _():
        for i in range(4):
            panel = gram.at[pl.ds(128 * i, 128), pl.ds(128 * i, BLOCK - 128 * i)]
            remote(panel, panel, usend.at[i], urecv.at[i], (me, rep + 1)).wait_send()

    for copy in store:
        copy.wait()


def pass_on(*refs):
    sources, results, held, sems = refs[:4], refs[4:8], refs[8:12], refs[12]
    arriving, leaving = [], []
    for i in range(4):
        half = sources[i].shape[0] // 2
        for h in range(2):
            rows = pl.ds(h * half, half)
            arriving.append(pltpu.make_async_copy(sources[i].at[rows], held[i].at[rows], sems.at[2 * i + h, 0]))
            leaving.append(pltpu.make_async_copy(held[i].at[rows], results[i].at[rows], sems.at[2 * i + h, 1]))
    for copy in arriving:
        copy.start()
    for come, go in zip(arriving, leaving):
        come.wait()
        go.start()
    for copy in leaving:
        copy.wait()


def shards(gradients, moments, second_moments, factors, owner_of, slot_order):
    anywhere = pl.BlockSpec(memory_space=pl.ANY)
    blocks = pltpu.VMEM((BLOCKS, 4, 128), f32)
    chunks2 = pltpu.VMEM((2 * OWNERS, 4, 128), f32)
    smem = pl.BlockSpec(memory_space=pltpu.SMEM)
    part = jax.ShapeDtypeStruct(gradients.shape, f32)
    chunks = lambda n: pltpu.VMEM((n, OWNERS, 4, 128), f32)
    halves = lambda n: pltpu.VMEM((n, 64, 2, 4, 128), f32)
    square = pltpu.VMEM((BLOCK, BLOCK), f32)
    dma = pltpu.SemaphoreType.DMA
    regular = pltpu.SemaphoreType.REGULAR
    out_shape = (part, part, part, jax.ShapeDtypeStruct((BLOCK, BLOCK), f32))
    results = pl.pallas_call(
        kernel,
        out_shape=out_shape,
        in_specs=[smem, smem] + [anywhere] * 4,
        out_specs=(anywhere,) * 4,
        scratch_shapes=[
            blocks, blocks, blocks, square, blocks, blocks, blocks, square, pltpu.SMEM((BLOCKS,), jnp.int32),
            chunks(2), halves(4), square, square, halves(4), halves(2), chunks2, square, square,
            pltpu.VMEM((1, 256), f32), pltpu.VMEM((256, 128), f32),
            pltpu.VMEM((16, 1, 256), f32), pltpu.VMEM((8, 1, 256), f32), pltpu.VMEM((4, 1, 256), f32),
            regular, regular, regular, regular, regular, regular, regular,
            dma, dma((4,)), dma((2,)), dma((2,)), dma((4,)), dma((4,)), dma, dma((2, 2)), dma, dma, dma((4,)), dma((3,)),
            dma((4,)), dma((4,)),
        ],
        compiler_params=pltpu.CompilerParams(
            collective_id=0, has_side_effects=True, vmem_limit_bytes=56 << 20
        ),
    )(slot_order.T, owner_of, gradients, moments, second_moments, factors.reshape(BLOCK, BLOCK))
    direction, new_m, new_v, new_f = pl.pallas_call(
        pass_on,
        out_shape=out_shape,
        in_specs=[anywhere] * 4,
        out_specs=(anywhere,) * 4,
        scratch_shapes=[blocks, blocks, blocks, square, dma((8, 2))],
    )(*results)
    return direction, new_m, new_v, new_f[None, None]


def solution(mesh):
    split_blocks = P(None, "fsdp", "rep")
    return jax.shard_map(
        shards,
        mesh=mesh,
        in_specs=(split_blocks, split_blocks, split_blocks, P("fsdp", "rep", None, None), P(), P()),
        out_specs=(split_blocks, split_blocks, split_blocks, P("fsdp", "rep", None, None)),
        check_vma=False,
    )
```
